32 devices in a mesh: re: 2 (over x), rp: 8 (over z, core), mode: 2 (over y).
Axes of the slice: x: 2, y: 2, z: 4, core: 2. Of those that a mesh axis runs over, the one named last changes fastest.
Arguments:
- coupling: float32 [2, 16, 8, 120, 576], P(None, 're', 'rp', 'mode'), may hold values from -0.5 to 0.5
- electron_cells: int32 [16, 3], replicated, may hold values from -6 to 6
- phonon_cells: int32 [8, 3], replicated, may hold values from -3 to 3
- kpoint_index: int32 [4, 3], replicated, may hold values from 0 to 15
- qpoint_index: int32 [8, 3], replicated, may hold values from 0 to 15
- eigenvectors: float32 [8, 2, 120, 120], P('rp', None, 'mode'), may hold values from -0.5 to 0.5
- frequencies: float32 [8, 120], P('rp', 'mode'), may hold values from 0.25 to 2
Outputs:
- mode_coupling: float32 [120, 8, 4, 2, 576], P('mode', 'rp', 're')
The draws below stay inside these ranges and needn't reach their ends.
All inputs are finite; a program needn't handle non-finite values.
Results may differ from the reference program's by a relative error of at most 0.00007.
Values sent between devices are 32-bit elements; how exact they have to be, the bound alone decides.
A program may use at most 64 MiB of HBM per device.

```python
import math
import jax
import jax.numpy as jnp
from jax import lax

P_SIZE = 576
MODES = 120
KG = 16
NRE = 16
NRP = 8
NK = 4
NQ = 8


def touch_ends(result, key, smallest, high):
    longest = result.shape.index(max(result.shape))
    spots = []
    for shift in (0, 1):
        where = [jax.random.randint(jax.random.fold_in(key, axis), (), 0, length) for axis, length in enumerate(result.shape)]
        where[longest] = (where[longest] + shift) % result.shape[longest]
        spots.append(tuple(where))
    return result.at[spots[0]].set(smallest).at[spots[1]].set(high)


def steps_of(rng, extent, cuts, low, high):
    gain = 1.0
    for axis_at, parts in cuts:
        heights = jax.random.uniform(jax.random.fold_in(jax.random.fold_in(rng, 6), axis_at), (parts,), jnp.float32, low / len(cuts), high / len(cuts))
        gain = gain * jnp.repeat(jnp.exp(heights), extent[axis_at] // parts).reshape((-1,) + (1,) * (len(extent) - 1 - axis_at))
    return gain


def gaussian(rng, shape, scale, reach, shards=(), dtype=jnp.bfloat16):
    level = steps_of(rng, shape, shards, -0.22, 0.18) if shards else 1.0
    values = jax.random.normal(rng, shape, jnp.float32) * scale * level
    return jnp.minimum(jnp.maximum(values, -reach), reach).astype(dtype)


def setup_inputs(seed: int = 0) -> dict:
    keys = jax.random.split(jax.random.key(seed), 8)
    return {
        "coupling": gaussian(keys[0], (2, NRE, NRP, MODES, P_SIZE), (NRE * NRP) ** -0.5, 0.5, ((1, 2), (2, 8), (3, 2)), jnp.float32),
        "electron_cells": touch_ends(jax.random.randint(keys[1], (NRE, 3), -6, 7), jax.random.fold_in(keys[1], 1), -6, 6).astype(jnp.int32),
        "phonon_cells": touch_ends(jax.random.randint(keys[2], (NRP, 3), -3, 4), jax.random.fold_in(keys[2], 1), -3, 3).astype(jnp.int32),
        "kpoint_index": touch_ends(jax.random.randint(keys[3], (NK, 3), 0, KG), jax.random.fold_in(keys[3], 1), 0, KG - 1).astype(jnp.int32),
        "qpoint_index": touch_ends(jax.random.randint(keys[4], (NQ, 3), 0, KG), jax.random.fold_in(keys[4], 1), 0, KG - 1).astype(jnp.int32),
        "eigenvectors": gaussian(keys[5], (NQ, 2, MODES, MODES), MODES ** -0.5, 0.5, ((0, 8), (2, 2)), jnp.float32),
        "frequencies": jnp.clip(jnp.exp(math.log(2.0) - 2.0794415 * jax.random.uniform(keys[6], (NQ, MODES), jnp.float32) ** steps_of(keys[6], (NQ, MODES), ((0, 8), (1, 2)), -0.2, 0.2)), 0.25, 2.0),
    }


def phases(points, cells):
    turns = lax.optimization_barrier(jnp.sum(points[:, None, :] * cells[None, :, :], axis=-1)) % KG
    angle = turns.astype(jnp.float32) * (2.0 * 3.141592653589793 / KG)
    return (jnp.cos(angle), jnp.sin(angle))

def reference(coupling, electron_cells, phonon_cells, kpoint_index, qpoint_index, eigenvectors, frequencies):
    hp = lax.Precision.HIGHEST
    cos_e, sin_e = phases(kpoint_index, electron_cells)
    real_part = coupling[0].reshape(NRE, -1)
    imag_part = coupling[1].reshape(NRE, -1)
    bk_real = jnp.dot(cos_e, real_part, precision=hp) - jnp.dot(sin_e, imag_part, precision=hp)
    bk_imag = jnp.dot(cos_e, imag_part, precision=hp) + jnp.dot(sin_e, real_part, precision=hp)
    bk_real = bk_real.reshape(NK, NRP, MODES, P_SIZE)
    bk_imag = bk_imag.reshape(NK, NRP, MODES, P_SIZE)
    cos_p, sin_p = phases(qpoint_index, phonon_cells)
    kq_real = jnp.einsum('qs,kscp->qkcp', cos_p, bk_real, precision=hp) - jnp.einsum('qs,kscp->qkcp', sin_p, bk_imag, precision=hp)
    kq_imag = jnp.einsum('qs,kscp->qkcp', cos_p, bk_imag, precision=hp) + jnp.einsum('qs,kscp->qkcp', sin_p, bk_real, precision=hp)
    vec_real = eigenvectors[:, 0]
    vec_imag = eigenvectors[:, 1]
    out_real = jnp.einsum('qkcp,qcn->nqkp', kq_real, vec_real, precision=hp) - jnp.einsum('qkcp,qcn->nqkp', kq_imag, vec_imag, precision=hp)
    out_imag = jnp.einsum('qkcp,qcn->nqkp', kq_real, vec_imag, precision=hp) + jnp.einsum('qkcp,qcn->nqkp', kq_imag, vec_real, precision=hp)
    factor = lax.rsqrt(2.0 * frequencies).T[:, :, None, None]
    return jnp.stack([out_real * factor, out_imag * factor], axis=3)
```

```python
import functools

import jax
import jax.numpy as jnp
from jax import lax
from jax.experimental import pallas as pl
from jax.experimental.pallas import tpu as pltpu
from jax.sharding import PartitionSpec as P

KG = 16
CORES = 2
LANES = 128
CHUNKS = 3
MESH = pl.DeviceIdType.MESH


def phases(points, cells):
    turns = jnp.sum(points[:, None, :] * cells[None, :, :], axis=-1) % KG
    angle = turns.astype(jnp.float32) * (2.0 * 3.141592653589793 / KG)
    return (jnp.cos(angle), jnp.sin(angle))


def row_blocks(rows, step):
    return [(r, min(r + step, rows)) for r in range(0, rows, step)]


def pieces_of(chunk, width, pairs):
    found = []
    at = chunk * width
    end = at + width
    while at < end:
        k = at // pairs
        stop = min(end, (k + 1) * pairs)
        found.append((k, at - k * pairs, stop - k * pairs, at - chunk * width))
        at = stop
    return found


def kernel(
    sizes, coupling, cos_e, sin_e, cos_p, sin_p, turn, out,
    xout, xin, raw, sumout, sumin, mine, sibout, sibin, packed, yout, yin,
    xs, xr, rs, rr, ss, sr, bs, br, ys, yr,
):
    n_re, n_rp, n_mode, chunks, width = sizes
    re_local, modes, pairs = coupling.shape[1], coupling.shape[3], coupling.shape[4]
    k_local = out.shape[0]
    pad = raw.shape[3]
    half = n_rp // CORES // 2
    me_re, me_rp, me_mode = lax.axis_index("re"), lax.axis_index("rp"), lax.axis_index("mode")
    chip, core = me_rp // CORES, me_rp % CORES
    side = jnp.where(chip >= half, 1, 0)
    depth = jnp.where(side == 1, chip - half, half - 1 - chip)

    def chip_at(d, s):
        return jnp.where(s == 1, half + d, half - 1 - d)

    inner = jnp.where(depth == 0, chip_at(0, 1 - side), chip_at(depth - 1, side)) * CORES + core
    outer = chip_at(jnp.minimum(depth + 1, half - 1), side) * CORES + core
    sibling = chip * CORES + 1 - core
    re_peers = [lax.rem(me_re + d, n_re) for d in range(1, n_re)]
    mode_peers = [lax.rem(me_mode + d, n_mode) for d in range(1, n_mode)]

    def remote(src, dst, send, recv, where):
        return pltpu.make_async_remote_copy(
            src_ref=src, dst_ref=dst, send_sem=send, recv_sem=recv,
            device_id=where, device_id_type=MESH,
        )

    def x_copy(d, j):
        return remote(xout.at[d, j], xin.at[d, j], xs.at[d, j], xr.at[d, j], {"re": re_peers[d]})

    def raw_copy(tt, i, j):
        to = half + i if tt == 0 else i + 1
        return remote(raw.at[i, j], raw.at[to, j], rs.at[i, j], rr.at[to, j], {"rp": inner})

    def raw_arrival(i, j):
        return remote(raw.at[i, j], raw.at[i, j], rs.at[0, j], rr.at[i, j], {"rp": inner})

    def sum_copy(i, c, j):
        return remote(
            sumout.at[i, c, j], sumin.at[i, c, j], ss.at[i, c, j], sr.at[i, c, j], {"rp": outer}
        )

    def sum_arrival(i, c, j):
        return remote(
            sumin.at[i, c, j], sumin.at[i, c, j], ss.at[0, c, j], sr.at[i, c, j], {"rp": outer}
        )

    def sib_copy(j):
        return remote(sibout.at[j], sibin.at[j], bs.at[j], br.at[j], {"rp": sibling})

    def y_copy(d, j):
        return remote(
            yout.at[mode_peers[d], j], yin.at[d, j], ys.at[d, j], yr.at[d, j],
            {"mode": mode_peers[d]},
        )

    barrier = pltpu.get_barrier_semaphore()

    def greet(where):
        pl.semaphore_signal(barrier, inc=1, device_id=where, device_id_type=MESH)

    for p in re_peers:
        greet({"re": p})
    for p in mode_peers:
        greet({"mode": p})
    greet({"rp": sibling})
    greet({"rp": inner})

    @pl.when(depth < half - 1)
    def _():
        greet({"rp": outer})

    friends = n_re - 1 + n_mode - 1 + 2
    pl.semaphore_wait(barrier, friends + jnp.where(depth < half - 1, 1, 0))

    def electron(owner, j, dst):
        for k, p0, p1, at in pieces_of(j, width, pairs):
            row = owner * k_local + k
            for r0, r1 in row_blocks(modes, 32):
                real = imag = None
                for r in range(re_local):
                    col = me_re * re_local + r
                    c, s = cos_e[row, col], sin_e[row, col]
                    a = coupling[0, r, 0, r0:r1, p0:p1]
                    b = coupling[1, r, 0, r0:r1, p0:p1]
                    x, y = c * a - s * b, c * b + s * a
                    real = x if real is None else real + x
                    imag = y if imag is None else imag + y
                dst[0, r0:r1, at:at + p1 - p0] = real
                dst[1, r0:r1, at:at + p1 - p0] = imag

    def phonon(dst, q, terms, start):
        for r0, r1 in row_blocks(modes, 32):
            real = imag = None
            if start is not None:
                real, imag = start[0, r0:r1, :], start[1, r0:r1, :]
            for src, s_chip in terms:
                s_at = s_chip * CORES + core
                c, s = cos_p[q, s_at], sin_p[q, s_at]
                a, b = src[0, r0:r1, :], src[1, r0:r1, :]
                x, y = c * a - s * b, c * b + s * a
                real = x if real is None else real + x
                imag = y if imag is None else imag + y
            dst[0, r0:r1, :] = real
            dst[1, r0:r1, :] = imag

    for j in range(chunks):
        for d in range(n_re - 1):
            electron(re_peers[d], j, xout.at[d, j])
            x_copy(d, j).start()
    for j in range(chunks):
        electron(me_re, j, raw.at[0, j])
    packed[...] = jnp.zeros_like(packed)

    def x_stage(j):
        for d in range(n_re - 1):
            x_copy(d, j).wait_recv()
        for r0, r1 in row_blocks(modes, 32):
            for part in range(2):
                total = raw[0, j, part, r0:r1, :]
                for d in range(n_re - 1):
                    total = total + xin[d, j, part, r0:r1, :]
                raw[0, j, part, r0:r1, :] = total
        for tt in range(half):
            @pl.when(depth == tt)
            def _():
                raw_copy(tt, 0, j).start()

    def forward_stage(j):
        for tt in range(half - 1):
            @pl.when(depth == tt)
            def _():
                for i in range(1, half - tt):
                    raw_arrival(i, j).wait_recv()
                    raw_copy(tt, i, j).start()

    def z_stage(j):
        for tt in range(half):
            @pl.when(depth == tt)
            def _():
                own = (raw.at[0, j], chip)
                outside = [(raw.at[i, j], chip_at(tt + i, side)) for i in range(1, half - tt)]
                if tt == 0:
                    for i in range(half):
                        raw_arrival(half + i, j).wait_recv()
                    across = [(raw.at[half + i, j], chip_at(i, 1 - side)) for i in range(half)]
                else:
                    for i in range(half - tt):
                        for c in range(CORES):
                            sum_arrival(i, c, j).wait_recv()
                    across = []
                for i in range(half - 1 - tt):
                    for c in range(CORES):
                        q = chip_at(tt + 1 + i, side) * CORES + c
                        start = None if tt == 0 else sumin.at[i + 1, c, j]
                        phonon(sumout.at[i, c, j], q, [own] + across, start)
                        sum_copy(i, c, j).start()
                for dst, c in ((sibout, 1 - core), (mine, core)):
                    start = None if tt == 0 else sumin.at[0, c, j]
                    phonon(dst.at[j], chip * CORES + c, [own] + across + outside, start)
                    if dst is sibout:
                        sib_copy(j).start()

    def mode_stage(j):
        sib_copy(j).wait_recv()
        for part in range(2):
            packed[part * pad:part * pad + modes, :] = (
                mine[j, part, :modes, :] + sibin[j, part, :modes, :]
            )
        turned = jnp.dot(
            turn[...], packed[...], precision=lax.Precision.HIGHEST,
            preferred_element_type=jnp.float32,
        )
        yout[:, j] = turned.reshape(n_mode, 2, pad, width)
        for d in range(n_mode - 1):
            y_copy(d, j).start()

    def out_stage(j):
        for d in range(n_mode - 1):
            y_copy(d, j).wait_recv()
        for part in range(2):
            total = yout[me_mode, j, part]
            for d in range(n_mode - 1):
                total = total + yin[d, j, part]
            for k, p0, p1, at in pieces_of(j, width, pairs):
                out[k, part, :, p0:p1] = total[:modes, at:at + p1 - p0]

    for j in range(chunks + 1):
        if j < chunks:
            x_stage(j)
        if j >= 1:
            forward_stage(j - 1)
    for j in range(chunks + 2):
        if j < chunks:
            z_stage(j)
        if 1 <= j <= chunks:
            mode_stage(j - 1)
        if j >= 2:
            out_stage(j - 2)

    for j in range(chunks):
        for d in range(n_re - 1):
            x_copy(d, j).wait_send()
        sib_copy(j).wait_send()
        for d in range(n_mode - 1):
            y_copy(d, j).wait_send()
        for tt in range(half):
            @pl.when(depth == tt)
            def _():
                for i in range(half - tt):
                    raw_copy(tt, i, j).wait_send()
                for i in range(half - 1 - tt):
                    for c in range(CORES):
                        sum_copy(i, c, j).wait_send()


def shards(
    coupling, electron_cells, phonon_cells, kpoint_index, qpoint_index, eigenvectors, frequencies
):
    n_re, n_rp, n_mode = lax.axis_size("re"), lax.axis_size("rp"), lax.axis_size("mode")
    modes, pairs = coupling.shape[3], coupling.shape[4]
    k_local = kpoint_index.shape[0] // n_re
    columns = k_local * pairs
    chunks = CHUNKS if columns % (CHUNKS * LANES) == 0 else 1
    width = columns // chunks
    pad = -(-modes // 8) * 8
    half = n_rp // CORES // 2
    cos_e, sin_e = phases(kpoint_index, electron_cells)
    cos_p, sin_p = phases(qpoint_index, phonon_cells)
    vec = eigenvectors[0].reshape(2, modes, n_mode, modes)
    vec = jnp.pad(vec, ((0, 0), (0, pad - modes), (0, 0), (0, pad - modes)))
    vec = vec.transpose(0, 2, 3, 1)
    upper = jnp.concatenate([vec[0], -vec[1]], axis=-1)
    lower = jnp.concatenate([vec[1], vec[0]], axis=-1)
    turn = jnp.stack([upper, lower], axis=1).reshape(n_mode * 2 * pad, 2 * pad)

    block = (2, pad, width)
    smem = pl.BlockSpec(memory_space=pltpu.SMEM)
    vmem = pl.BlockSpec(memory_space=pltpu.VMEM)
    peers, others = max(n_re - 1, 1), max(n_mode - 1, 1)
    dma = pltpu.SemaphoreType.DMA
    rest = max(half - 1, 1)
    f32 = jnp.float32
    rotated = pl.pallas_call(
        functools.partial(kernel, (n_re, n_rp, n_mode, chunks, width)),
        out_shape=jax.ShapeDtypeStruct((k_local, 2, modes, pairs), f32),
        in_specs=[vmem, smem, smem, smem, smem, vmem],
        out_specs=vmem,
        scratch_shapes=[
            pltpu.VMEM((peers, chunks) + block, f32),
            pltpu.VMEM((peers, chunks) + block, f32),
            pltpu.VMEM((2 * half, chunks) + block, f32),
            pltpu.VMEM((rest, CORES, chunks) + block, f32),
            pltpu.VMEM((half, CORES, chunks) + block, f32),
            pltpu.VMEM((chunks,) + block, f32),
            pltpu.VMEM((chunks,) + block, f32),
            pltpu.VMEM((chunks,) + block, f32),
            pltpu.VMEM((2 * pad, width), f32),
            pltpu.VMEM((n_mode, chunks) + block, f32),
            pltpu.VMEM((others, chunks) + block, f32),
            dma((peers, chunks)), dma((peers, chunks)),
            dma((half, chunks)), dma((2 * half, chunks)),
            dma((rest, CORES, chunks)), dma((half, CORES, chunks)),
            dma((chunks,)), dma((chunks,)),
            dma((others, chunks)), dma((others, chunks)),
        ],
        compiler_params=pltpu.CompilerParams(
            collective_id=0, has_side_effects=True, vmem_limit_bytes=48 * 1024 * 1024
        ),
    )(coupling, cos_e, sin_e, cos_p, sin_p, turn)
    factor = lax.rsqrt(2.0 * frequencies).T[:, :, None, None, None]
    return rotated.transpose(2, 0, 1, 3)[:, None] * factor


def solution(mesh):
    placed = (
        P(None, "re", "rp", "mode", None),
        P(),
        P(),
        P(),
        P(),
        P("rp", None, "mode", None),
        P("rp", "mode"),
    )
    return jax.shard_map(
        shards,
        mesh=mesh,
        in_specs=placed,
        out_specs=P("mode", "rp", "re", None, None),
        check_vma=False,
    )
```

```python
import functools

import jax
import jax.numpy as jnp
import numpy as np
from jax import lax
from jax.experimental import pallas as pl
from jax.experimental.pallas import tpu as pltpu
from jax.sharding import PartitionSpec as P

KG = 16
CORES = 2
LANES = 128
CHUNKS = 9
MESH = pl.DeviceIdType.MESH


def segments(modes):
    base = modes // 8 * 8
    left = modes - base
    shared = 0 if left == 0 else (8 if 2 * left <= 8 else 16)
    rows = [(0, 0, base, 0), (1, 0, base, base + shared)]
    if left:
        rows += [(0, base, modes, base), (1, base, modes, base + shared // 2)]
    return base, left, shared, rows


def pieces_of(chunk, width, pairs):
    found = []
    at = chunk * width
    end = at + width
    while at < end:
        k = at // pairs
        stop = min(end, (k + 1) * pairs)
        found.append((k, at - k * pairs, stop - k * pairs, at - chunk * width))
        at = stop
    return found


def kernel(
    sizes, coupling, electron_cells, phonon_cells, kpoints, qpoints, roots, vectors, out,
    held, cos_e, sin_e, cos_p, sin_p, square, turn,
    xout, xin, raw, sumout, sumin, mine, sibout, sibin, packed, yout, yin,
    load, xs, xr, rs, rr, ss, sr, bs, br, ys, yr,
):
    n_re, n_rp, n_mode, chunks, width = sizes
    re_local, modes, pairs = coupling.shape[1], coupling.shape[3], coupling.shape[4]
    k_local = out.shape[0]
    base, left, shared, rows = segments(modes)
    tall = 2 * base + shared
    half = n_rp // CORES // 2
    me_re, me_rp, me_mode = lax.axis_index("re"), lax.axis_index("rp"), lax.axis_index("mode")
    chip, core = me_rp // CORES, me_rp % CORES
    side = jnp.where(chip >= half, 1, 0)
    depth = jnp.where(side == 1, chip - half, half - 1 - chip)

    fetch = pltpu.make_async_copy(coupling, held, load)
    fetch.start()

    def chip_at(d, s):
        return jnp.where(s == 1, half + d, half - 1 - d)

    inner = jnp.where(depth == 0, chip_at(0, 1 - side), chip_at(depth - 1, side)) * CORES + core
    outer = chip_at(jnp.minimum(depth + 1, half - 1), side) * CORES + core
    sibling = chip * CORES + 1 - core
    re_peers = [lax.rem(me_re + d, n_re) for d in range(1, n_re)]
    mode_peers = [lax.rem(me_mode + d, n_mode) for d in range(1, n_mode)]

    def remote(src, dst, send, recv, where):
        return pltpu.make_async_remote_copy(
            src_ref=src, dst_ref=dst, send_sem=send, recv_sem=recv,
            device_id=where, device_id_type=MESH,
        )

    def x_copy(d, j):
        return remote(xout.at[d, j], xin.at[d, j], xs.at[d, j], xr.at[d, j], {"re": re_peers[d]})

    def raw_copy(tt, i, j):
        to = half + i if tt == 0 else i + 1
        return remote(raw.at[i, j], raw.at[to, j], rs.at[i, j], rr.at[to, j], {"rp": inner})

    def raw_arrival(i, j):
        return remote(raw.at[i, j], raw.at[i, j], rs.at[0, j], rr.at[i, j], {"rp": inner})

    def sum_copy(i, j):
        return remote(sumout.at[i, j], sumin.at[i, j], ss.at[i, j], sr.at[i, j], {"rp": outer})

    def sum_arrival(i, j):
        return remote(sumin.at[i, j], sumin.at[i, j], ss.at[0, j], sr.at[i, j], {"rp": outer})

    def sib_copy(tt, j):
        some = pl.ds(0, half - tt)
        return remote(sibout.at[j, some], sibin.at[j, some], bs.at[j], br.at[j], {"rp": sibling})

    def y_copy(d, j):
        return remote(
            yout.at[mode_peers[d], j], yin.at[d, j], ys.at[d, j], yr.at[d, j],
            {"mode": mode_peers[d]},
        )

    barrier = pltpu.get_barrier_semaphore()

    def greet(where):
        pl.semaphore_signal(barrier, inc=1, device_id=where, device_id_type=MESH)

    for p in re_peers:
        greet({"re": p})
    for p in mode_peers:
        greet({"mode": p})
    greet({"rp": sibling})
    greet({"rp": inner})

    @pl.when(depth < half - 1)
    def _():
        greet({"rp": outer})

    def table(points, cells, first, count, cos_t, sin_t):
        for i in range(points.shape[0]):
            for s in range(count):
                turns = points[i, 0] * cells[first + s, 0]
                for axis in range(1, points.shape[1]):
                    turns = turns + points[i, axis] * cells[first + s, axis]
                cos_t[i, s] = roots[turns & (KG - 1)]
                sin_t[i, s] = roots[(turns + (KG - KG // 4)) & (KG - 1)]

    table(kpoints, electron_cells, me_re * re_local, re_local, cos_e, sin_e)

    friends = n_re - 1 + n_mode - 1 + 2
    pl.semaphore_wait(barrier, friends + jnp.where(depth < half - 1, 1, 0))
    fetch.wait()

    def electron(owner, j, dst):
        if left and 2 * left != shared:
            dst[base:base + shared, :] = jnp.zeros((shared, width), jnp.float32)
        spans = [(rows[0], rows[1])] + ([(rows[2], rows[3])] if left else [])
        for k, p0, p1, at in pieces_of(j, width, pairs):
            row = owner * k_local + k
            for (_, r0, r1, to_real), (_, _, _, to_imag) in spans:
                real = imag = None
                for r in range(re_local):
                    c, s = cos_e[row, r], sin_e[row, r]
                    a = held[0, r, 0, r0:r1, p0:p1]
                    b = held[1, r, 0, r0:r1, p0:p1]
                    x, y = c * a - s * b, c * b + s * a
                    real = x if real is None else real + x
                    imag = y if imag is None else imag + y
                dst[to_real:to_real + r1 - r0, at:at + p1 - p0] = real
                dst[to_imag:to_imag + r1 - r0, at:at + p1 - p0] = imag

    def phonon(dst, q, terms):
        factors = [(src, s_chip * CORES + core) for src, s_chip in terms]
        real = imag = both = None
        for src, s_at in factors:
            c, s = cos_p[q, s_at], sin_p[q, s_at]
            a, b = src[0:base, :], src[base + shared:tall, :]
            x, y = c * a - s * b, c * b + s * a
            real = x if real is None else real + x
            imag = y if imag is None else imag + y
        dst[0:base, :] = real
        dst[base + shared:tall, :] = imag
        if left:
            place = lax.broadcasted_iota(jnp.int32, (shared, width), 0)
            sign = jnp.where(place < shared // 2, -1.0, 1.0)
            for src, s_at in factors:
                c, s = cos_p[q, s_at], sin_p[q, s_at]
                t = src[base:base + shared, :]
                x = c * t + s * (sign * pltpu.roll(t, shared // 2, 0))
                both = x if both is None else both + x
            dst[base:base + shared, :] = both

    for j in range(chunks):
        for d in range(n_re - 1):
            electron(re_peers[d], j, xout.at[d, j])
            x_copy(d, j).start()

    table(qpoints, phonon_cells, 0, n_rp, cos_p, sin_p)

    def x_stage(j):
        electron(me_re, j, raw.at[0, j])
        for d in range(n_re - 1):
            x_copy(d, j).wait_recv()
        total = raw[0, j]
        for d in range(n_re - 1):
            total = total + xin[d, j]
        raw[0, j] = total
        for tt in range(half):
            @pl.when(depth == tt)
            def _():
                raw_copy(tt, 0, j).start()

    def forward_stage(j):
        for tt in range(half - 1):
            @pl.when(depth == tt)
            def _():
                for i in range(1, half - tt):
                    raw_arrival(i, j).wait_recv()
                    raw_copy(tt, i, j).start()

    def turn_stage():
        square[...] = jnp.zeros_like(square)
        n_all = vectors.shape[3]
        flipped = []
        for part in range(2):
            square[0:modes, 0:n_all] = vectors[0, part]
            flipped.append(jnp.transpose(square[...]))
        for m in range(n_mode):
            turn[m] = jnp.zeros(turn.shape[1:], jnp.float32)
            for to, n0, n1, at_n in rows:
                for come, c0, c1, at_c in rows:
                    block = flipped[0 if to == come else 1]
                    block = block[m * modes + n0:m * modes + n1, c0:c1]
                    if to < come:
                        block = -block
                    turn[m, at_n:at_n + n1 - n0, at_c:at_c + c1 - c0] = block

    def z_stage(j):
        for tt in range(half):
            @pl.when(depth == tt)
            def _():
                own = (raw.at[0, j], chip)
                outside = [(raw.at[i, j], chip_at(tt + i, side)) for i in range(1, half - tt)]
                across = []
                if tt == 0:
                    for i in range(half):
                        raw_arrival(half + i, j).wait_recv()
                    across = [(raw.at[half + i, j], chip_at(i, 1 - side)) for i in range(half)]
                for dst, c in ((sibout, 1 - core), (mine, core)):
                    for i in range(half - tt):
                        q = chip_at(tt + i, side) * CORES + c
                        phonon(dst.at[j, i], q, [own] + across + (outside if i == 0 else []))
                    if dst is sibout:
                        sib_copy(tt, j).start()

    def sum_stage(j):
        for tt in range(half):
            @pl.when(depth == tt)
            def _():
                sib_copy(tt, j).wait_recv()
                if tt > 0:
                    for i in range(half - tt):
                        sum_arrival(i, j).wait_recv()
                for i in list(range(1, half - tt)) + [0]:
                    total = mine[j, i] + sibin[j, i]
                    if tt > 0:
                        total = total + sumin[i, j]
                    if i == 0:
                        packed[j] = total
                    else:
                        sumout[i - 1, j] = total
                        sum_copy(i - 1, j).start()

    def mode_stage(j):
        for m in range(n_mode):
            yout[m, j] = jnp.dot(
                turn[m], packed[j], precision=lax.Precision.HIGHEST,
                preferred_element_type=jnp.float32,
            )
        for d in range(n_mode - 1):
            y_copy(d, j).start()

    def out_stage(j):
        for d in range(n_mode - 1):
            y_copy(d, j).wait_recv()
        total = yout[me_mode, j]
        for d in range(n_mode - 1):
            total = total + yin[d, j]
        for k, p0, p1, at in pieces_of(j, width, pairs):
            for part, n0, n1, at_n in rows:
                out[k, part, n0:n1, p0:p1] = total[at_n:at_n + n1 - n0, at:at + p1 - p0]

    xs_done = forwarded = 0
    turn_ready = False
    for j in range(chunks + 3):
        until = min(2 * j + 5, chunks)
        while xs_done < until:
            x_stage(xs_done)
            xs_done += 1
            while forwarded < xs_done - 1:
                forward_stage(forwarded)
                forwarded += 1
        if xs_done == chunks and forwarded < chunks:
            forward_stage(forwarded)
            forwarded += 1
        if not turn_ready:
            turn_stage()
            turn_ready = True
        if j < chunks:
            z_stage(j)
        if 1 <= j <= chunks:
            sum_stage(j - 1)
            mode_stage(j - 1)
        if 3 <= j:
            out_stage(j - 3)

    for j in range(chunks):
        for d in range(n_re - 1):
            x_copy(d, j).wait_send()
        for d in range(n_mode - 1):
            y_copy(d, j).wait_send()
        for tt in range(half):
            @pl.when(depth == tt)
            def _():
                sib_copy(tt, j).wait_send()
                for i in range(half - tt):
                    raw_copy(tt, i, j).wait_send()
                for i in range(half - 1 - tt):
                    sum_copy(i, j).wait_send()


def shards(
    coupling, electron_cells, phonon_cells, kpoint_index, qpoint_index, eigenvectors, frequencies
):
    n_re, n_rp, n_mode = lax.axis_size("re"), lax.axis_size("rp"), lax.axis_size("mode")
    modes, pairs = coupling.shape[3], coupling.shape[4]
    k_all, q_all = kpoint_index.shape[0], qpoint_index.shape[0]
    k_local = k_all // n_re
    columns = k_local * pairs
    chunks = CHUNKS if columns % (CHUNKS * LANES) == 0 else 1
    width = columns // chunks
    base, _, shared, _ = segments(modes)
    tall = 2 * base + shared
    half = n_rp // CORES // 2
    side = -(-eigenvectors.shape[3] // LANES) * LANES
    roots = jnp.asarray(np.cos(np.arange(KG) * (2.0 * np.pi / KG)).astype(np.float32))

    block = (tall, width)
    smem = pl.BlockSpec(memory_space=pltpu.SMEM)
    vmem = pl.BlockSpec(memory_space=pltpu.VMEM)
    peers, others = max(n_re - 1, 1), max(n_mode - 1, 1)
    dma = pltpu.SemaphoreType.DMA
    rest = max(half - 1, 1)
    f32 = jnp.float32
    rotated = pl.pallas_call(
        functools.partial(kernel, (n_re, n_rp, n_mode, chunks, width)),
        out_shape=jax.ShapeDtypeStruct((k_local, 2, modes, pairs), f32),
        in_specs=[pl.BlockSpec(memory_space=pl.ANY)] + [smem] * 5 + [vmem],
        out_specs=vmem,
        scratch_shapes=[
            pltpu.VMEM(coupling.shape, f32),
            pltpu.SMEM((k_all, coupling.shape[1]), f32),
            pltpu.SMEM((k_all, coupling.shape[1]), f32),
            pltpu.SMEM((q_all, n_rp), f32),
            pltpu.SMEM((q_all, n_rp), f32),
            pltpu.VMEM((side, side), f32),
            pltpu.VMEM((n_mode, tall, tall), f32),
            pltpu.VMEM((peers, chunks) + block, f32),
            pltpu.VMEM((peers, chunks) + block, f32),
            pltpu.VMEM((2 * half, chunks) + block, f32),
            pltpu.VMEM((rest, chunks) + block, f32),
            pltpu.VMEM((half, chunks) + block, f32),
            pltpu.VMEM((chunks, half) + block, f32),
            pltpu.VMEM((chunks, half) + block, f32),
            pltpu.VMEM((chunks, half) + block, f32),
            pltpu.VMEM((chunks,) + block, f32),
            pltpu.VMEM((n_mode, chunks) + block, f32),
            pltpu.VMEM((others, chunks) + block, f32),
            dma, dma((peers, chunks)), dma((peers, chunks)),
            dma((half, chunks)), dma((2 * half, chunks)),
            dma((rest, chunks)), dma((half, chunks)),
            dma((chunks,)), dma((chunks,)),
            dma((others, chunks)), dma((others, chunks)),
        ],
        compiler_params=pltpu.CompilerParams(
            collective_id=0, has_side_effects=True, vmem_limit_bytes=56 * 1024 * 1024
        ),
    )(coupling, electron_cells, phonon_cells, kpoint_index, qpoint_index, roots, eigenvectors)
    factor = lax.rsqrt(2.0 * frequencies).T[:, :, None, None, None]
    return rotated.transpose(2, 0, 1, 3)[:, None] * factor


def solution(mesh):
    placed = (
        P(None, "re", "rp", "mode", None),
        P(),
        P(),
        P(),
        P(),
        P("rp", None, "mode", None),
        P("rp", "mode"),
    )
    return jax.shard_map(
        shards,
        mesh=mesh,
        in_specs=placed,
        out_specs=P("mode", "rp", "re", None, None),
        check_vma=False,
    )
```

```python
import functools

import jax
import jax.numpy as jnp
import numpy as np
from jax import lax
from jax.experimental import pallas as pl
from jax.experimental.pallas import tpu as pltpu
from jax.sharding import PartitionSpec as P

KG = 16
CORES = 2
LANES = 128
CHUNKS = 9
LEAD = 4
MESH = pl.DeviceIdType.MESH


def segments(modes):
    base = modes // 8 * 8
    left = modes - base
    shared = 0 if left == 0 else (8 if 2 * left <= 8 else 16)
    rows = [(0, 0, base, 0), (1, 0, base, base + shared)]
    if left:
        rows += [(0, base, modes, base), (1, base, modes, base + shared // 2)]
    return base, left, shared, rows


def split(x):
    high = x.astype(jnp.bfloat16)
    return high, (x - high.astype(jnp.float32)).astype(jnp.bfloat16)


def pieces_of(chunk, width, pairs):
    found = []
    at = chunk * width
    end = at + width
    while at < end:
        k = at // pairs
        stop = min(end, (k + 1) * pairs)
        found.append((k, at - k * pairs, stop - k * pairs, at - chunk * width))
        at = stop
    return found


def kernel(
    sizes, coupling, electron_cells, phonon_cells, kpoints, qpoints, roots, vectors, out,
    held, cos_e, sin_e, cos_p, sin_p, square, turn,
    xout, xin, raw, sumout, sumin, mine, sibout, sibin, packed, yout, yin,
    load, xs, xr, rs, rr, ss, sr, bs, br, ys, yr,
):
    n_re, n_rp, n_mode, chunks, width = sizes
    re_local, modes, pairs = coupling.shape[1], coupling.shape[2], coupling.shape[4]
    k_local = out.shape[0]
    base, left, shared, rows = segments(modes)
    tall = 2 * base + shared
    half = n_rp // CORES // 2
    me_re, me_rp, me_mode = lax.axis_index("re"), lax.axis_index("rp"), lax.axis_index("mode")
    chip, core = me_rp // CORES, me_rp % CORES
    side = jnp.where(chip >= half, 1, 0)
    depth = jnp.where(side == 1, chip - half, half - 1 - chip)

    fetch = pltpu.make_async_copy(coupling.at[:, :, :, 0, :], held, load)
    fetch.start()

    def chip_at(d, s):
        return jnp.where(s == 1, half + d, half - 1 - d)

    inner = jnp.where(depth == 0, chip_at(0, 1 - side), chip_at(depth - 1, side)) * CORES + core
    outer = chip_at(jnp.minimum(depth + 1, half - 1), side) * CORES + core
    sibling = chip * CORES + 1 - core
    re_peers = [lax.rem(me_re + d, n_re) for d in range(1, n_re)]
    mode_peers = [lax.rem(me_mode + d, n_mode) for d in range(1, n_mode)]

    def remote(src, dst, send, recv, where):
        return pltpu.make_async_remote_copy(
            src_ref=src, dst_ref=dst, send_sem=send, recv_sem=recv,
            device_id=where, device_id_type=MESH,
        )

    def x_copy(d, j):
        return remote(xout.at[d, j], xin.at[d, j], xs.at[d, j], xr.at[d, j], {"re": re_peers[d]})

    def raw_copy(tt, i, j):
        to = half + i if tt == 0 else i + 1
        return remote(raw.at[i, j], raw.at[to, j], rs.at[i, j], rr.at[to, j], {"rp": inner})

    def raw_arrival(i, j):
        return remote(raw.at[i, j], raw.at[i, j], rs.at[0, j], rr.at[i, j], {"rp": inner})

    def sum_copy(i, j):
        return remote(sumout.at[i, j], sumin.at[i, j], ss.at[i, j], sr.at[i, j], {"rp": outer})

    def sum_arrival(i, j):
        return remote(sumin.at[i, j], sumin.at[i, j], ss.at[0, j], sr.at[i, j], {"rp": outer})

    def sib_copy(tt, j):
        some = pl.ds(0, half - tt)
        return remote(sibout.at[j, some], sibin.at[j, some], bs.at[j], br.at[j], {"rp": sibling})

    def y_copy(d, j):
        return remote(
            yout.at[mode_peers[d], j], yin.at[d, j], ys.at[d, j], yr.at[d, j],
            {"mode": mode_peers[d]},
        )

    barrier = pltpu.get_barrier_semaphore()

    def greet(where):
        pl.semaphore_signal(barrier, inc=1, device_id=where, device_id_type=MESH)

    for p in re_peers:
        greet({"re": p})
    for p in mode_peers:
        greet({"mode": p})
    greet({"rp": sibling})
    greet({"rp": inner})

    @pl.when(depth < half - 1)
    def _():
        greet({"rp": outer})

    def table(points, point, cells, first, count, cos_t, sin_t):
        for i in range(points):
            for s in range(count):
                turns = point(i, 0) * cells[0, first + s]
                for axis in range(1, cells.shape[0]):
                    turns = turns + point(i, axis) * cells[axis, first + s]
                cos_t[i, s] = roots[turns & (KG - 1)]
                sin_t[i, s] = roots[(turns + (KG - KG // 4)) & (KG - 1)]

    table(cos_e.shape[0], lambda i, a: kpoints[i, a], electron_cells, me_re * re_local, re_local, cos_e, sin_e)

    friends = n_re - 1 + n_mode - 1 + 2
    pl.semaphore_wait(barrier, friends + jnp.where(depth < half - 1, 1, 0))
    fetch.wait()

    def electron(owner, j, dst):
        if left and 2 * left != shared:
            dst[base:base + shared, :] = jnp.zeros((shared, width), jnp.float32)
        spans = [(rows[0], rows[1])] + ([(rows[2], rows[3])] if left else [])
        for k, p0, p1, at in pieces_of(j, width, pairs):
            row = owner * k_local + k
            for (_, r0, r1, to_real), (_, _, _, to_imag) in spans:
                real = imag = None
                for r in range(re_local):
                    c, s = cos_e[row, r], sin_e[row, r]
                    a = held[0, r, r0:r1, p0:p1]
                    b = held[1, r, r0:r1, p0:p1]
                    x, y = c * a - s * b, c * b + s * a
                    real = x if real is None else real + x
                    imag = y if imag is None else imag + y
                dst[to_real:to_real + r1 - r0, at:at + p1 - p0] = real
                dst[to_imag:to_imag + r1 - r0, at:at + p1 - p0] = imag

    def phonon(dst, q, terms):
        factors = [(src, s_chip * CORES + core) for src, s_chip in terms]
        real = imag = both = None
        for src, s_at in factors:
            c, s = cos_p[q, s_at], sin_p[q, s_at]
            a, b = src[0:base, :], src[base + shared:tall, :]
            x, y = c * a - s * b, c * b + s * a
            real = x if real is None else real + x
            imag = y if imag is None else imag + y
        dst[0:base, :] = real
        dst[base + shared:tall, :] = imag
        if left:
            place = lax.broadcasted_iota(jnp.int32, (shared, width), 0)
            sign = jnp.where(place < shared // 2, -1.0, 1.0)
            for src, s_at in factors:
                c, s = cos_p[q, s_at], sin_p[q, s_at]
                t = src[base:base + shared, :]
                x = c * t + s * (sign * pltpu.roll(t, shared // 2, 0))
                both = x if both is None else both + x
            dst[base:base + shared, :] = both

    def peer_stage(j):
        for d in range(n_re - 1):
            electron(re_peers[d], j, xout.at[d, j])
            x_copy(d, j).start()

    for j in range(min(LEAD, chunks)):
        peer_stage(j)

    table(cos_p.shape[0], lambda i, a: qpoints[a, i], phonon_cells, 0, n_rp, cos_p, sin_p)

    def x_stage(j):
        electron(me_re, j, raw.at[0, j])
        for d in range(n_re - 1):
            x_copy(d, j).wait_recv()
        total = raw[0, j]
        for d in range(n_re - 1):
            total = total + xin[d, j]
        raw[0, j] = total
        for tt in range(half):
            @pl.when(depth == tt)
            def _():
                raw_copy(tt, 0, j).start()
        if j + LEAD < chunks:
            peer_stage(j + LEAD)

    def forward_stage(j):
        for tt in range(half - 1):
            @pl.when(depth == tt)
            def _():
                for i in range(1, half - tt):
                    raw_arrival(i, j).wait_recv()
                    raw_copy(tt, i, j).start()

    def turn_stage():
        square[...] = jnp.zeros_like(square)
        n_all = vectors.shape[3]
        flipped = []
        for part in range(2):
            square[0:modes, 0:n_all] = vectors[0, :, part, :]
            flipped.append(jnp.transpose(square[...]))
        for m in range(n_mode):
            turn[m] = jnp.zeros(turn.shape[1:], jnp.float32)
            for to, n0, n1, at_n in rows:
                for come, c0, c1, at_c in rows:
                    block = flipped[0 if to == come else 1]
                    block = block[m * modes + n0:m * modes + n1, c0:c1]
                    if to < come:
                        block = -block
                    turn[m, at_n:at_n + n1 - n0, at_c:at_c + c1 - c0] = block

    def z_stage(j):
        for tt in range(half):
            @pl.when(depth == tt)
            def _():
                own = (raw.at[0, j], chip)
                outside = [(raw.at[i, j], chip_at(tt + i, side)) for i in range(1, half - tt)]
                across = []
                if tt == 0:
                    for i in range(half):
                        raw_arrival(half + i, j).wait_recv()
                    across = [(raw.at[half + i, j], chip_at(i, 1 - side)) for i in range(half)]
                for dst, c in ((sibout, 1 - core), (mine, core)):
                    for i in range(half - tt):
                        q = chip_at(tt + i, side) * CORES + c
                        phonon(dst.at[j, i], q, [own] + across + (outside if i == 0 else []))
                    if dst is sibout:
                        sib_copy(tt, j).start()

    def sum_stage(j):
        for tt in range(half):
            @pl.when(depth == tt)
            def _():
                sib_copy(tt, j).wait_recv()
                if tt > 0:
                    for i in range(half - tt):
                        sum_arrival(i, j).wait_recv()
                for i in list(range(1, half - tt)) + [0]:
                    total = mine[j, i] + sibin[j, i]
                    if tt > 0:
                        total = total + sumin[i, j]
                    if i == 0:
                        packed[j] = total
                    else:
                        sumout[i - 1, j] = total
                        sum_copy(i - 1, j).start()

    def mode_stage(j):
        w_high, w_low = split(turn[...].reshape(n_mode * tall, tall))
        x_high, x_low = split(packed[j])

        def product(w, x):
            return jnp.dot(w, x, preferred_element_type=jnp.float32)

        turned = product(w_high, x_low) + product(w_low, x_high) + product(w_high, x_high)
        yout[:, j] = turned.reshape(n_mode, tall, width)
        for d in range(n_mode - 1):
            y_copy(d, j).start()

    def out_stage(j):
        for d in range(n_mode - 1):
            y_copy(d, j).wait_recv()
        total = yout[me_mode, j]
        for d in range(n_mode - 1):
            total = total + yin[d, j]
        for k, p0, p1, at in pieces_of(j, width, pairs):
            for part, n0, n1, at_n in rows:
                out[k, part, n0:n1, p0:p1] = total[at_n:at_n + n1 - n0, at:at + p1 - p0]

    xs_done = forwarded = 0
    turn_ready = False
    for j in range(chunks + 3):
        until = min(3 * j + 6, chunks)
        while xs_done < until:
            x_stage(xs_done)
            xs_done += 1
            while forwarded < xs_done - 1:
                forward_stage(forwarded)
                forwarded += 1
        if xs_done == chunks and forwarded < chunks:
            forward_stage(forwarded)
            forwarded += 1
        if not turn_ready:
            turn_stage()
            turn_ready = True
        if j < chunks:
            z_stage(j)
        if 1 <= j <= chunks:
            sum_stage(j - 1)
            mode_stage(j - 1)
        if 3 <= j:
            out_stage(j - 3)

    for j in range(chunks):
        for d in range(n_re - 1):
            x_copy(d, j).wait_send()
        for d in range(n_mode - 1):
            y_copy(d, j).wait_send()
        for tt in range(half):
            @pl.when(depth == tt)
            def _():
                sib_copy(tt, j).wait_send()
                for i in range(half - tt):
                    raw_copy(tt, i, j).wait_send()
                for i in range(half - 1 - tt):
                    sum_copy(i, j).wait_send()


def shards(
    coupling, electron_cells, phonon_cells, kpoint_index, qpoint_index, eigenvectors, frequencies
):
    n_re, n_rp, n_mode = lax.axis_size("re"), lax.axis_size("rp"), lax.axis_size("mode")
    modes, pairs = coupling.shape[3], coupling.shape[4]
    k_all, q_all = kpoint_index.shape[0], qpoint_index.shape[0]
    k_local = k_all // n_re
    columns = k_local * pairs
    chunks = CHUNKS if columns % (CHUNKS * LANES) == 0 else 1
    width = columns // chunks
    base, _, shared, _ = segments(modes)
    tall = 2 * base + shared
    half = n_rp // CORES // 2
    side = -(-eigenvectors.shape[3] // LANES) * LANES
    roots = jnp.asarray(np.cos(np.arange(KG) * (2.0 * np.pi / KG)).astype(np.float32))

    block = (tall, width)
    smem = pl.BlockSpec(memory_space=pltpu.SMEM)
    vmem = pl.BlockSpec(memory_space=pltpu.VMEM)
    peers, others = max(n_re - 1, 1), max(n_mode - 1, 1)
    dma = pltpu.SemaphoreType.DMA
    rest = max(half - 1, 1)
    f32 = jnp.float32
    rotated = pl.pallas_call(
        functools.partial(kernel, (n_re, n_rp, n_mode, chunks, width)),
        out_shape=jax.ShapeDtypeStruct((k_local, 2, modes, pairs), f32),
        in_specs=[pl.BlockSpec(memory_space=pl.ANY)] + [smem] * 5 + [vmem],
        out_specs=vmem,
        scratch_shapes=[
            pltpu.VMEM((2, coupling.shape[1], modes, pairs), f32),
            pltpu.SMEM((k_all, coupling.shape[1]), f32),
            pltpu.SMEM((k_all, coupling.shape[1]), f32),
            pltpu.SMEM((q_all, n_rp), f32),
            pltpu.SMEM((q_all, n_rp), f32),
            pltpu.VMEM((side, side), f32),
            pltpu.VMEM((n_mode, tall, tall), f32),
            pltpu.VMEM((peers, chunks) + block, f32),
            pltpu.VMEM((peers, chunks) + block, f32),
            pltpu.VMEM((2 * half, chunks) + block, f32),
            pltpu.VMEM((rest, chunks) + block, f32),
            pltpu.VMEM((half, chunks) + block, f32),
            pltpu.VMEM((chunks, half) + block, f32),
            pltpu.VMEM((chunks, half) + block, f32),
            pltpu.VMEM((chunks, half) + block, f32),
            pltpu.VMEM((chunks,) + block, f32),
            pltpu.VMEM((n_mode, chunks) + block, f32),
            pltpu.VMEM((others, chunks) + block, f32),
            dma, dma((peers, chunks)), dma((peers, chunks)),
            dma((half, chunks)), dma((2 * half, chunks)),
            dma((rest, chunks)), dma((half, chunks)),
            dma((chunks,)), dma((chunks,)),
            dma((others, chunks)), dma((others, chunks)),
        ],
        compiler_params=pltpu.CompilerParams(
            collective_id=0, has_side_effects=True, vmem_limit_bytes=56 * 1024 * 1024
        ),
    )(
        coupling.transpose(0, 1, 3, 2, 4), electron_cells.T, phonon_cells.T, kpoint_index,
        qpoint_index.T, roots, eigenvectors.transpose(0, 2, 1, 3),
    )
    factor = lax.rsqrt(2.0 * frequencies).T[:, :, None, None, None]
    return rotated.transpose(2, 0, 1, 3)[:, None] * factor


def solution(mesh):
    placed = (
        P(None, "re", "rp", "mode", None),
        P(),
        P(),
        P(),
        P(),
        P("rp", None, "mode", None),
        P("rp", "mode"),
    )
    return jax.shard_map(
        shards,
        mesh=mesh,
        in_specs=placed,
        out_specs=P("mode", "rp", "re", None, None),
        check_vma=False,
    )
```

```python
import functools

import jax
import jax.numpy as jnp
import numpy as np
from jax import lax
from jax.experimental import pallas as pl
from jax.experimental.pallas import tpu as pltpu
from jax.sharding import PartitionSpec as P

KG = 16
CORES = 2
LANES = 128
CHUNKS = 9
LEAD = 4
MESH = pl.DeviceIdType.MESH


def segments(modes):
    base = modes // 8 * 8
    left = modes - base
    shared = 0 if left == 0 else (8 if 2 * left <= 8 else 16)
    rows = [(0, 0, base, 0), (1, 0, base, base + shared)]
    if left:
        rows += [(0, base, modes, base), (1, base, modes, base + shared // 2)]
    return base, left, shared, rows


def split(x):
    high = x.astype(jnp.bfloat16)
    return high, (x - high.astype(jnp.float32)).astype(jnp.bfloat16)


def pieces_of(chunk, width, pairs):
    found = []
    at = chunk * width
    end = at + width
    while at < end:
        k = at // pairs
        stop = min(end, (k + 1) * pairs)
        found.append((k, at - k * pairs, stop - k * pairs, at - chunk * width))
        at = stop
    return found


def kernel(
    sizes, coupling, electron_cells, phonon_cells, kpoints, qpoints, roots, vectors, out,
    held, cos_e, sin_e, cos_p, sin_p, square, turn,
    xout, xin, raw, sumout, sumin, mine, sibout, sibin, packed, yout, yin,
    load, xs, xr, rs, rr, ss, sr, bs, br, ys, yr,
):
    n_re, n_rp, n_mode, chunks, width = sizes
    re_local, modes, pairs = coupling.shape[1], coupling.shape[2], coupling.shape[4]
    k_local = out.shape[1]
    base, left, shared, rows = segments(modes)
    tall = 2 * base + shared
    half = n_rp // CORES // 2
    me_re, me_rp, me_mode = lax.axis_index("re"), lax.axis_index("rp"), lax.axis_index("mode")
    chip, core = me_rp // CORES, me_rp % CORES
    side = jnp.where(chip >= half, 1, 0)
    depth = jnp.where(side == 1, chip - half, half - 1 - chip)

    fetches = []
    for p in range(0, pairs, LANES):
        span = pl.ds(p, min(LANES, pairs - p))
        fetches.append(pltpu.make_async_copy(
            coupling.at[:, :, :, 0, span], held.at[:, :, :, span], load.at[len(fetches)]
        ))
    for fetch in fetches:
        fetch.start()
    fetched = []

    def chip_at(d, s):
        return jnp.where(s == 1, half + d, half - 1 - d)

    inner = jnp.where(depth == 0, chip_at(0, 1 - side), chip_at(depth - 1, side)) * CORES + core
    outer = chip_at(jnp.minimum(depth + 1, half - 1), side) * CORES + core
    sibling = chip * CORES + 1 - core
    re_peers = [lax.rem(me_re + d, n_re) for d in range(1, n_re)]
    mode_peers = [lax.rem(me_mode + d, n_mode) for d in range(1, n_mode)]

    def remote(src, dst, send, recv, where):
        return pltpu.make_async_remote_copy(
            src_ref=src, dst_ref=dst, send_sem=send, recv_sem=recv,
            device_id=where, device_id_type=MESH,
        )

    def x_copy(d, j):
        return remote(xout.at[d, j], xin.at[d, j], xs.at[d, j], xr.at[d, j], {"re": re_peers[d]})

    def raw_copy(tt, i, j):
        to = half + i if tt == 0 else i + 1
        return remote(raw.at[i, j], raw.at[to, j], rs.at[i, j], rr.at[to, j], {"rp": inner})

    def raw_arrival(i, j):
        return remote(raw.at[i, j], raw.at[i, j], rs.at[0, j], rr.at[i, j], {"rp": inner})

    def sum_copy(i, j):
        return remote(sumout.at[i, j], sumin.at[i, j], ss.at[i, j], sr.at[i, j], {"rp": outer})

    def sum_arrival(i, j):
        return remote(sumin.at[i, j], sumin.at[i, j], ss.at[0, j], sr.at[i, j], {"rp": outer})

    def sib_copy(tt, j):
        some = pl.ds(0, half - tt)
        return remote(sibout.at[j, some], sibin.at[j, some], bs.at[j], br.at[j], {"rp": sibling})

    def y_copy(d, j):
        return remote(
            yout.at[mode_peers[d], j], yin.at[d, j], ys.at[d, j], yr.at[d, j],
            {"mode": mode_peers[d]},
        )

    barrier = pltpu.get_barrier_semaphore()

    def greet(where):
        pl.semaphore_signal(barrier, inc=1, device_id=where, device_id_type=MESH)

    for p in re_peers:
        greet({"re": p})
    for p in mode_peers:
        greet({"mode": p})
    greet({"rp": sibling})
    greet({"rp": inner})

    @pl.when(depth < half - 1)
    def _():
        greet({"rp": outer})

    def table(points, point, cells, first, count, cos_t, sin_t):
        for i in range(points):
            for s in range(count):
                turns = point(i, 0) * cells[0, first + s]
                for axis in range(1, cells.shape[0]):
                    turns = turns + point(i, axis) * cells[axis, first + s]
                cos_t[i, s] = roots[turns & (KG - 1)]
                sin_t[i, s] = roots[(turns + (KG - KG // 4)) & (KG - 1)]

    table(cos_e.shape[0], lambda i, a: kpoints[i, a], electron_cells, me_re * re_local, re_local, cos_e, sin_e)

    friends = n_re - 1 + n_mode - 1 + 2
    pl.semaphore_wait(barrier, friends + jnp.where(depth < half - 1, 1, 0))

    def electron(owner, j, dst):
        if left and 2 * left != shared:
            dst[base:base + shared, :] = jnp.zeros((shared, width), jnp.float32)
        spans = [(rows[0], rows[1])] + ([(rows[2], rows[3])] if left else [])
        for k, p0, p1, at in pieces_of(j, width, pairs):
            row = owner * k_local + k
            while len(fetched) * LANES < p1:
                fetches[len(fetched)].wait()
                fetched.append(p1)
            for (_, r0, r1, to_real), (_, _, _, to_imag) in spans:
                real = imag = None
                for r in range(re_local):
                    c, s = cos_e[row, r], sin_e[row, r]
                    a = held[0, r, r0:r1, p0:p1]
                    b = held[1, r, r0:r1, p0:p1]
                    x, y = c * a - s * b, c * b + s * a
                    real = x if real is None else real + x
                    imag = y if imag is None else imag + y
                dst[to_real:to_real + r1 - r0, at:at + p1 - p0] = real
                dst[to_imag:to_imag + r1 - r0, at:at + p1 - p0] = imag

    def phonon(dst, q, terms):
        factors = [(src, s_chip * CORES + core) for src, s_chip in terms]
        real = imag = both = None
        for src, s_at in factors:
            c, s = cos_p[q, s_at], sin_p[q, s_at]
            a, b = src[0:base, :], src[base + shared:tall, :]
            x, y = c * a - s * b, c * b + s * a
            real = x if real is None else real + x
            imag = y if imag is None else imag + y
        dst[0:base, :] = real
        dst[base + shared:tall, :] = imag
        if left:
            place = lax.broadcasted_iota(jnp.int32, (shared, width), 0)
            sign = jnp.where(place < shared // 2, -1.0, 1.0)
            for src, s_at in factors:
                c, s = cos_p[q, s_at], sin_p[q, s_at]
                t = src[base:base + shared, :]
                x = c * t + s * (sign * pltpu.roll(t, shared // 2, 0))
                both = x if both is None else both + x
            dst[base:base + shared, :] = both

    def peer_stage(j):
        for d in range(n_re - 1):
            electron(re_peers[d], j, xout.at[d, j])
            x_copy(d, j).start()

    for j in range(min(LEAD, chunks)):
        peer_stage(j)

    table(cos_p.shape[0], lambda i, a: qpoints[a, i], phonon_cells, 0, n_rp, cos_p, sin_p)

    def x_stage(j):
        electron(me_re, j, raw.at[0, j])
        for d in range(n_re - 1):
            x_copy(d, j).wait_recv()
        total = raw[0, j]
        for d in range(n_re - 1):
            total = total + xin[d, j]
        raw[0, j] = total
        for tt in range(half):
            @pl.when(depth == tt)
            def _():
                raw_copy(tt, 0, j).start()
        if j + LEAD < chunks:
            peer_stage(j + LEAD)

    def forward_stage(j):
        for tt in range(half - 1):
            @pl.when(depth == tt)
            def _():
                for i in range(1, half - tt):
                    raw_arrival(i, j).wait_recv()
                    raw_copy(tt, i, j).start()

    def turn_stage():
        square[...] = jnp.zeros_like(square)
        n_all = vectors.shape[3]
        flipped = []
        for part in range(2):
            square[0:modes, 0:n_all] = vectors[0, :, part, :]
            flipped.append(jnp.transpose(square[...]))
        for m in range(n_mode):
            turn[m] = jnp.zeros(turn.shape[1:], jnp.float32)
            for to, n0, n1, at_n in rows:
                for come, c0, c1, at_c in rows:
                    block = flipped[0 if to == come else 1]
                    block = block[m * modes + n0:m * modes + n1, c0:c1]
                    if to < come:
                        block = -block
                    turn[m, at_n:at_n + n1 - n0, at_c:at_c + c1 - c0] = block

    def z_stage(j):
        for tt in range(half):
            @pl.when(depth == tt)
            def _():
                own = (raw.at[0, j], chip)
                outside = [(raw.at[i, j], chip_at(tt + i, side)) for i in range(1, half - tt)]
                across = []
                if tt == 0:
                    for i in range(half):
                        raw_arrival(half + i, j).wait_recv()
                    across = [(raw.at[half + i, j], chip_at(i, 1 - side)) for i in range(half)]
                for dst, c in ((sibout, 1 - core), (mine, core)):
                    for i in range(half - tt):
                        q = chip_at(tt + i, side) * CORES + c
                        phonon(dst.at[j, i], q, [own] + across + (outside if i == 0 else []))
                    if dst is sibout:
                        sib_copy(tt, j).start()

    def sum_stage(j):
        for tt in range(half):
            @pl.when(depth == tt)
            def _():
                sib_copy(tt, j).wait_recv()
                if tt > 0:
                    for i in range(half - tt):
                        sum_arrival(i, j).wait_recv()
                for i in list(range(1, half - tt)) + [0]:
                    total = mine[j, i] + sibin[j, i]
                    if tt > 0:
                        total = total + sumin[i, j]
                    if i == 0:
                        packed[j] = total
                    else:
                        sumout[i - 1, j] = total
                        sum_copy(i - 1, j).start()

    def mode_stage(j):
        w_high, w_low = split(turn[...].reshape(n_mode * tall, tall))
        x_high, x_low = split(packed[j])

        def product(w, x):
            return jnp.dot(w, x, preferred_element_type=jnp.float32)

        turned = product(w_high, x_low) + product(w_low, x_high) + product(w_high, x_high)
        yout[:, j] = turned.reshape(n_mode, tall, width)
        for d in range(n_mode - 1):
            y_copy(d, j).start()

    def out_stage(j):
        for d in range(n_mode - 1):
            y_copy(d, j).wait_recv()
        total = yout[me_mode, j]
        for d in range(n_mode - 1):
            total = total + yin[d, j]
        for k, p0, p1, at in pieces_of(j, width, pairs):
            for part, n0, n1, at_n in rows:
                out[n0:n1, k, part, p0:p1] = total[at_n:at_n + n1 - n0, at:at + p1 - p0]

    xs_done = forwarded = 0
    turn_ready = False
    for j in range(chunks + 3):
        until = min(3 * j + 6, chunks)
        while xs_done < until:
            x_stage(xs_done)
            xs_done += 1
            while forwarded < xs_done - 1:
                forward_stage(forwarded)
                forwarded += 1
        if xs_done == chunks and forwarded < chunks:
            forward_stage(forwarded)
            forwarded += 1
        if not turn_ready:
            turn_stage()
            turn_ready = True
        if j < chunks:
            z_stage(j)
        if 1 <= j <= chunks:
            sum_stage(j - 1)
            mode_stage(j - 1)
        if 3 <= j:
            out_stage(j - 3)

    for j in range(chunks):
        for d in range(n_re - 1):
            x_copy(d, j).wait_send()
        for d in range(n_mode - 1):
            y_copy(d, j).wait_send()
        for tt in range(half):
            @pl.when(depth == tt)
            def _():
                sib_copy(tt, j).wait_send()
                for i in range(half - tt):
                    raw_copy(tt, i, j).wait_send()
                for i in range(half - 1 - tt):
                    sum_copy(i, j).wait_send()


def shards(
    coupling, electron_cells, phonon_cells, kpoint_index, qpoint_index, eigenvectors, frequencies
):
    n_re, n_rp, n_mode = lax.axis_size("re"), lax.axis_size("rp"), lax.axis_size("mode")
    modes, pairs = coupling.shape[3], coupling.shape[4]
    k_all, q_all = kpoint_index.shape[0], qpoint_index.shape[0]
    k_local = k_all // n_re
    columns = k_local * pairs
    chunks = CHUNKS if columns % (CHUNKS * LANES) == 0 else 1
    width = columns // chunks
    base, _, shared, _ = segments(modes)
    tall = 2 * base + shared
    half = n_rp // CORES // 2
    side = -(-eigenvectors.shape[3] // LANES) * LANES
    roots = jnp.asarray(np.cos(np.arange(KG) * (2.0 * np.pi / KG)).astype(np.float32))

    block = (tall, width)
    smem = pl.BlockSpec(memory_space=pltpu.SMEM)
    vmem = pl.BlockSpec(memory_space=pltpu.VMEM)
    peers, others = max(n_re - 1, 1), max(n_mode - 1, 1)
    dma = pltpu.SemaphoreType.DMA
    rest = max(half - 1, 1)
    f32 = jnp.float32
    rotated = pl.pallas_call(
        functools.partial(kernel, (n_re, n_rp, n_mode, chunks, width)),
        out_shape=jax.ShapeDtypeStruct((modes, k_local, 2, pairs), f32),
        in_specs=[pl.BlockSpec(memory_space=pl.ANY)] + [smem] * 5 + [vmem],
        out_specs=vmem,
        scratch_shapes=[
            pltpu.VMEM((2, coupling.shape[1], modes, pairs), f32),
            pltpu.SMEM((k_all, coupling.shape[1]), f32),
            pltpu.SMEM((k_all, coupling.shape[1]), f32),
            pltpu.SMEM((q_all, n_rp), f32),
            pltpu.SMEM((q_all, n_rp), f32),
            pltpu.VMEM((side, side), f32),
            pltpu.VMEM((n_mode, tall, tall), f32),
            pltpu.VMEM((peers, chunks) + block, f32),
            pltpu.VMEM((peers, chunks) + block, f32),
            pltpu.VMEM((2 * half, chunks) + block, f32),
            pltpu.VMEM((rest, chunks) + block, f32),
            pltpu.VMEM((half, chunks) + block, f32),
            pltpu.VMEM((chunks, half) + block, f32),
            pltpu.VMEM((chunks, half) + block, f32),
            pltpu.VMEM((chunks, half) + block, f32),
            pltpu.VMEM((chunks,) + block, f32),
            pltpu.VMEM((n_mode, chunks) + block, f32),
            pltpu.VMEM((others, chunks) + block, f32),
            dma((-(-pairs // LANES),)), dma((peers, chunks)), dma((peers, chunks)),
            dma((half, chunks)), dma((2 * half, chunks)),
            dma((rest, chunks)), dma((half, chunks)),
            dma((chunks,)), dma((chunks,)),
            dma((others, chunks)), dma((others, chunks)),
        ],
        compiler_params=pltpu.CompilerParams(
            collective_id=0, has_side_effects=True, vmem_limit_bytes=56 * 1024 * 1024
        ),
    )(
        coupling.transpose(0, 1, 3, 2, 4), electron_cells.T, phonon_cells.T, kpoint_index,
        qpoint_index.T, roots, eigenvectors.transpose(0, 2, 1, 3),
    )
    factor = lax.rsqrt(2.0 * frequencies).T[:, :, None, None, None]
    return rotated[:, None] * factor


def solution(mesh):
    placed = (
        P(None, "re", "rp", "mode", None),
        P(),
        P(),
        P(),
        P(),
        P("rp", None, "mode", None),
        P("rp", "mode"),
    )
    return jax.shard_map(
        shards,
        mesh=mesh,
        in_specs=placed,
        out_specs=P("mode", "rp", "re", None, None),
        check_vma=False,
    )
```

```python
import functools

import jax
import jax.numpy as jnp
import numpy as np
from jax import lax
from jax.experimental import pallas as pl
from jax.experimental.pallas import tpu as pltpu
from jax.sharding import PartitionSpec as P

KG = 16
CORES = 2
LANES = 128
CHUNKS = 9
LEAD = 4
FLIGHT = 2
MESH = pl.DeviceIdType.MESH


def segments(modes):
    base = modes // 8 * 8
    left = modes - base
    shared = 0 if left == 0 else (8 if 2 * left <= 8 else 16)
    rows = [(0, 0, base, 0), (1, 0, base, base + shared)]
    if left:
        rows += [(0, base, modes, base), (1, base, modes, base + shared // 2)]
    return base, left, shared, rows


def split(x):
    high = x.astype(jnp.bfloat16)
    return high, (x - high.astype(jnp.float32)).astype(jnp.bfloat16)


def pieces_of(chunk, width, pairs):
    found = []
    at = chunk * width
    end = at + width
    while at < end:
        k = at // pairs
        stop = min(end, (k + 1) * pairs)
        found.append((k, at - k * pairs, stop - k * pairs, at - chunk * width))
        at = stop
    return found


def kernel(
    sizes, coupling, electron_cells, phonon_cells, kpoints, qpoints, roots, vectors, out,
    held, cos_e, sin_e, cos_p, sin_p, square, turn,
    xout, xin, raw, sumout, sumin, mine, sibout, sibin, packed, yout, yin,
    load, xs, xr, rs, rr, ss, sr, bs, br, ys, yr,
):
    n_re, n_rp, n_mode, chunks, width = sizes
    re_local, modes, pairs = coupling.shape[1], coupling.shape[2], coupling.shape[4]
    k_local = out.shape[1]
    base, left, shared, rows = segments(modes)
    tall = 2 * base + shared
    half = n_rp // CORES // 2
    me_re, me_rp, me_mode = lax.axis_index("re"), lax.axis_index("rp"), lax.axis_index("mode")
    chip, core = me_rp // CORES, me_rp % CORES
    side = jnp.where(chip >= half, 1, 0)
    depth = jnp.where(side == 1, chip - half, half - 1 - chip)

    fetches = []
    for p in range(0, pairs, LANES):
        span = pl.ds(p, min(LANES, pairs - p))
        fetches.append(pltpu.make_async_copy(
            coupling.at[:, :, :, 0, span], held.at[:, :, :, span], load.at[len(fetches)]
        ))
    for fetch in fetches:
        fetch.start()
    fetched = []

    def chip_at(d, s):
        return jnp.where(s == 1, half + d, half - 1 - d)

    inner = jnp.where(depth == 0, chip_at(0, 1 - side), chip_at(depth - 1, side)) * CORES + core
    outer = chip_at(jnp.minimum(depth + 1, half - 1), side) * CORES + core
    sibling = chip * CORES + 1 - core
    re_peers = [lax.rem(me_re + d, n_re) for d in range(1, n_re)]
    mode_peers = [lax.rem(me_mode + d, n_mode) for d in range(1, n_mode)]

    def remote(src, dst, send, recv, where):
        return pltpu.make_async_remote_copy(
            src_ref=src, dst_ref=dst, send_sem=send, recv_sem=recv,
            device_id=where, device_id_type=MESH,
        )

    def x_copy(d, j):
        return remote(xout.at[d, j], xin.at[d, j], xs.at[d, j], xr.at[d, j], {"re": re_peers[d]})

    def raw_copy(tt, i, j):
        to = half + i if tt == 0 else i + 1
        return remote(raw.at[i, j], raw.at[to, j], rs.at[i, j], rr.at[to, j], {"rp": inner})

    def raw_arrival(i, j):
        return remote(raw.at[i, j], raw.at[i, j], rs.at[0, j], rr.at[i, j], {"rp": inner})

    def sum_copy(i, j):
        return remote(sumout.at[i, j], sumin.at[i, j], ss.at[i, j], sr.at[i, j], {"rp": outer})

    def sum_arrival(i, j):
        return remote(sumin.at[i, j], sumin.at[i, j], ss.at[0, j], sr.at[i, j], {"rp": outer})

    def sib_copy(tt, j):
        some = pl.ds(0, half - tt)
        return remote(sibout.at[j, some], sibin.at[j, some], bs.at[j], br.at[j], {"rp": sibling})

    def y_copy(d, j):
        return remote(
            yout.at[mode_peers[d], j], yin.at[d, j], ys.at[d, j], yr.at[d, j],
            {"mode": mode_peers[d]},
        )

    barrier = pltpu.get_barrier_semaphore()

    def greet(where):
        pl.semaphore_signal(barrier, inc=1, device_id=where, device_id_type=MESH)

    for p in re_peers:
        greet({"re": p})
    for p in mode_peers:
        greet({"mode": p})
    greet({"rp": sibling})
    greet({"rp": inner})

    @pl.when(depth < half - 1)
    def _():
        greet({"rp": outer})

    def table(points, point, cells, first, count, cos_t, sin_t):
        for i in range(points):
            for s in range(count):
                turns = point(i, 0) * cells[0, first + s]
                for axis in range(1, cells.shape[0]):
                    turns = turns + point(i, axis) * cells[axis, first + s]
                cos_t[i, s] = roots[turns & (KG - 1)]
                sin_t[i, s] = roots[(turns + (KG - KG // 4)) & (KG - 1)]

    table(cos_e.shape[0], lambda i, a: kpoints[i, a], electron_cells, me_re * re_local, re_local, cos_e, sin_e)

    friends = n_re - 1 + n_mode - 1 + 2
    pl.semaphore_wait(barrier, friends + jnp.where(depth < half - 1, 1, 0))

    def electron(owner, j, dst):
        if left and 2 * left != shared:
            dst[base:base + shared, :] = jnp.zeros((shared, width), jnp.float32)
        spans = [(rows[0], rows[1])] + ([(rows[2], rows[3])] if left else [])
        for k, p0, p1, at in pieces_of(j, width, pairs):
            row = owner * k_local + k
            while len(fetched) * LANES < p1:
                fetches[len(fetched)].wait()
                fetched.append(p1)
            for (_, r0, r1, to_real), (_, _, _, to_imag) in spans:
                real = imag = None
                for r in range(re_local):
                    c, s = cos_e[row, r], sin_e[row, r]
                    a = held[0, r, r0:r1, p0:p1]
                    b = held[1, r, r0:r1, p0:p1]
                    x, y = c * a - s * b, c * b + s * a
                    real = x if real is None else real + x
                    imag = y if imag is None else imag + y
                dst[to_real:to_real + r1 - r0, at:at + p1 - p0] = real
                dst[to_imag:to_imag + r1 - r0, at:at + p1 - p0] = imag

    def phonon(dst, q, terms):
        factors = [(src, s_chip * CORES + core) for src, s_chip in terms]
        real = imag = both = None
        for src, s_at in factors:
            c, s = cos_p[q, s_at], sin_p[q, s_at]
            a, b = src[0:base, :], src[base + shared:tall, :]
            x, y = c * a - s * b, c * b + s * a
            real = x if real is None else real + x
            imag = y if imag is None else imag + y
        dst[0:base, :] = real
        dst[base + shared:tall, :] = imag
        if left:
            place = lax.broadcasted_iota(jnp.int32, (shared, width), 0)
            sign = jnp.where(place < shared // 2, -1.0, 1.0)
            for src, s_at in factors:
                c, s = cos_p[q, s_at], sin_p[q, s_at]
                t = src[base:base + shared, :]
                x = c * t + s * (sign * pltpu.roll(t, shared // 2, 0))
                both = x if both is None else both + x
            dst[base:base + shared, :] = both

    def peer_stage(j):
        for d in range(n_re - 1):
            electron(re_peers[d], j, xout.at[d, j])
            x_copy(d, j).start()

    for j in range(min(LEAD, chunks)):
        peer_stage(j)

    table(cos_p.shape[0], lambda i, a: qpoints[a, i], phonon_cells, 0, n_rp, cos_p, sin_p)

    def x_stage(j):
        electron(me_re, j, raw.at[0, j])
        for d in range(n_re - 1):
            x_copy(d, j).wait_recv()
        total = raw[0, j]
        for d in range(n_re - 1):
            total = total + xin[d, j]
        raw[0, j] = total
        for tt in range(half):
            @pl.when(depth == tt)
            def _():
                if tt == 0 and j >= FLIGHT:
                    raw_copy(tt, 0, j - FLIGHT).wait_send()
                raw_copy(tt, 0, j).start()
        if j + LEAD < chunks:
            peer_stage(j + LEAD)

    def forward_stage(j):
        for tt in range(half - 1):
            @pl.when(depth == tt)
            def _():
                for i in range(1, half - tt):
                    raw_arrival(i, j).wait_recv()
                    if tt == 0 and j >= FLIGHT:
                        raw_copy(tt, i, j - FLIGHT).wait_send()
                    raw_copy(tt, i, j).start()

    def turn_stage():
        square[...] = jnp.zeros_like(square)
        n_all = vectors.shape[3]
        flipped = []
        for part in range(2):
            square[0:modes, 0:n_all] = vectors[0, :, part, :]
            flipped.append(jnp.transpose(square[...]))
        for m in range(n_mode):
            turn[m] = jnp.zeros(turn.shape[1:], jnp.float32)
            for to, n0, n1, at_n in rows:
                for come, c0, c1, at_c in rows:
                    block = flipped[0 if to == come else 1]
                    block = block[m * modes + n0:m * modes + n1, c0:c1]
                    if to < come:
                        block = -block
                    turn[m, at_n:at_n + n1 - n0, at_c:at_c + c1 - c0] = block

    def z_stage(j):
        for tt in range(half):
            @pl.when(depth == tt)
            def _():
                own = (raw.at[0, j], chip)
                outside = [(raw.at[i, j], chip_at(tt + i, side)) for i in range(1, half - tt)]
                across = []
                if tt == 0:
                    for i in range(half):
                        raw_arrival(half + i, j).wait_recv()
                    across = [(raw.at[half + i, j], chip_at(i, 1 - side)) for i in range(half)]
                for dst, c in ((sibout, 1 - core), (mine, core)):
                    for i in range(half - tt):
                        q = chip_at(tt + i, side) * CORES + c
                        phonon(dst.at[j, i], q, [own] + across + (outside if i == 0 else []))
                    if dst is sibout:
                        sib_copy(tt, j).start()

    def sum_stage(j):
        for tt in range(half):
            @pl.when(depth == tt)
            def _():
                sib_copy(tt, j).wait_recv()
                if tt > 0:
                    for i in range(half - tt):
                        sum_arrival(i, j).wait_recv()
                for i in list(range(1, half - tt)) + [0]:
                    total = mine[j, i] + sibin[j, i]
                    if tt > 0:
                        total = total + sumin[i, j]
                    if i == 0:
                        packed[j] = total
                    else:
                        sumout[i - 1, j] = total
                        sum_copy(i - 1, j).start()

    def mode_stage(j):
        w_high, w_low = split(turn[...].reshape(n_mode * tall, tall))
        x_high, x_low = split(packed[j])

        def product(w, x):
            return jnp.dot(w, x, preferred_element_type=jnp.float32)

        turned = product(w_high, x_low) + product(w_low, x_high) + product(w_high, x_high)
        yout[:, j] = turned.reshape(n_mode, tall, width)
        for d in range(n_mode - 1):
            y_copy(d, j).start()

    def out_stage(j):
        for d in range(n_mode - 1):
            y_copy(d, j).wait_recv()
        total = yout[me_mode, j]
        for d in range(n_mode - 1):
            total = total + yin[d, j]
        for k, p0, p1, at in pieces_of(j, width, pairs):
            for part, n0, n1, at_n in rows:
                out[n0:n1, k, part, p0:p1] = total[at_n:at_n + n1 - n0, at:at + p1 - p0]

    xs_done = forwarded = 0
    turn_ready = False
    for j in range(chunks + 3):
        until = min(j + 5, chunks)
        while xs_done < until:
            x_stage(xs_done)
            xs_done += 1
            while forwarded < xs_done - 1:
                forward_stage(forwarded)
                forwarded += 1
        if xs_done == chunks and forwarded < chunks:
            forward_stage(forwarded)
            forwarded += 1
        if not turn_ready:
            turn_stage()
            turn_ready = True
        if j < chunks:
            z_stage(j)
        if 1 <= j <= chunks:
            sum_stage(j - 1)
            mode_stage(j - 1)
        if 3 <= j:
            out_stage(j - 3)

    for j in range(chunks):
        for d in range(n_re - 1):
            x_copy(d, j).wait_send()
        for d in range(n_mode - 1):
            y_copy(d, j).wait_send()
        for tt in range(half):
            @pl.when(depth == tt)
            def _():
                sib_copy(tt, j).wait_send()
                for i in range(half - tt):
                    if tt > 0 or j + FLIGHT >= chunks:
                        raw_copy(tt, i, j).wait_send()
                for i in range(half - 1 - tt):
                    sum_copy(i, j).wait_send()


def shards(
    coupling, electron_cells, phonon_cells, kpoint_index, qpoint_index, eigenvectors, frequencies
):
    n_re, n_rp, n_mode = lax.axis_size("re"), lax.axis_size("rp"), lax.axis_size("mode")
    modes, pairs = coupling.shape[3], coupling.shape[4]
    k_all, q_all = kpoint_index.shape[0], qpoint_index.shape[0]
    k_local = k_all // n_re
    columns = k_local * pairs
    chunks = CHUNKS if columns % (CHUNKS * LANES) == 0 else 1
    width = columns // chunks
    base, _, shared, _ = segments(modes)
    tall = 2 * base + shared
    half = n_rp // CORES // 2
    side = -(-eigenvectors.shape[3] // LANES) * LANES
    roots = jnp.asarray(np.cos(np.arange(KG) * (2.0 * np.pi / KG)).astype(np.float32))

    block = (tall, width)
    smem = pl.BlockSpec(memory_space=pltpu.SMEM)
    vmem = pl.BlockSpec(memory_space=pltpu.VMEM)
    peers, others = max(n_re - 1, 1), max(n_mode - 1, 1)
    dma = pltpu.SemaphoreType.DMA
    rest = max(half - 1, 1)
    f32 = jnp.float32
    rotated = pl.pallas_call(
        functools.partial(kernel, (n_re, n_rp, n_mode, chunks, width)),
        out_shape=jax.ShapeDtypeStruct((modes, k_local, 2, pairs), f32),
        in_specs=[pl.BlockSpec(memory_space=pl.ANY)] + [smem] * 5 + [vmem],
        out_specs=vmem,
        scratch_shapes=[
            pltpu.VMEM((2, coupling.shape[1], modes, pairs), f32),
            pltpu.SMEM((k_all, coupling.shape[1]), f32),
            pltpu.SMEM((k_all, coupling.shape[1]), f32),
            pltpu.SMEM((q_all, n_rp), f32),
            pltpu.SMEM((q_all, n_rp), f32),
            pltpu.VMEM((side, side), f32),
            pltpu.VMEM((n_mode, tall, tall), f32),
            pltpu.VMEM((peers, chunks) + block, f32),
            pltpu.VMEM((peers, chunks) + block, f32),
            pltpu.VMEM((2 * half, chunks) + block, f32),
            pltpu.VMEM((rest, chunks) + block, f32),
            pltpu.VMEM((half, chunks) + block, f32),
            pltpu.VMEM((chunks, half) + block, f32),
            pltpu.VMEM((chunks, half) + block, f32),
            pltpu.VMEM((chunks, half) + block, f32),
            pltpu.VMEM((chunks,) + block, f32),
            pltpu.VMEM((n_mode, chunks) + block, f32),
            pltpu.VMEM((others, chunks) + block, f32),
            dma((-(-pairs // LANES),)), dma((peers, chunks)), dma((peers, chunks)),
            dma((half, chunks)), dma((2 * half, chunks)),
            dma((rest, chunks)), dma((half, chunks)),
            dma((chunks,)), dma((chunks,)),
            dma((others, chunks)), dma((others, chunks)),
        ],
        compiler_params=pltpu.CompilerParams(
            collective_id=0, has_side_effects=True, vmem_limit_bytes=56 * 1024 * 1024
        ),
    )(
        coupling.transpose(0, 1, 3, 2, 4), electron_cells.T, phonon_cells.T, kpoint_index,
        qpoint_index.T, roots, eigenvectors.transpose(0, 2, 1, 3),
    )
    factor = lax.rsqrt(2.0 * frequencies).T[:, :, None, None, None]
    return rotated[:, None] * factor


def solution(mesh):
    placed = (
        P(None, "re", "rp", "mode", None),
        P(),
        P(),
        P(),
        P(),
        P("rp", None, "mode", None),
        P("rp", "mode"),
    )
    return jax.shard_map(
        shards,
        mesh=mesh,
        in_specs=placed,
        out_specs=P("mode", "rp", "re", None, None),
        check_vma=False,
    )
```

```python
import functools

import jax
import jax.numpy as jnp
import numpy as np
from jax import lax
from jax.experimental import pallas as pl
from jax.experimental.pallas import tpu as pltpu
from jax.sharding import PartitionSpec as P

KG = 16
CORES = 2
LANES = 128
CHUNKS = 9
LEAD = 4
MESH = pl.DeviceIdType.MESH


def segments(modes):
    base = modes // 8 * 8
    left = modes - base
    shared = 0 if left == 0 else (8 if 2 * left <= 8 else 16)
    rows = [(0, 0, base, 0), (1, 0, base, base + shared)]
    if left:
        rows += [(0, base, modes, base), (1, base, modes, base + shared // 2)]
    return base, left, shared, rows


def split(x):
    high = x.astype(jnp.bfloat16)
    return high, (x - high.astype(jnp.float32)).astype(jnp.bfloat16)


def pieces_of(chunk, width, pairs):
    found = []
    at = chunk * width
    end = at + width
    while at < end:
        k = at // pairs
        stop = min(end, (k + 1) * pairs)
        found.append((k, at - k * pairs, stop - k * pairs, at - chunk * width))
        at = stop
    return found


def kernel(
    sizes, coupling, electron_cells, phonon_cells, kpoints, qpoints, roots, vectors, out,
    held, cos_e, sin_e, cos_p, sin_p, square, turn,
    xout, xin, raw, sumout, sumin, mine, sibout, sibin, packed, yout, yin,
    load, xs, xr, rs, rr, ss, sr, bs, br, ys, yr,
):
    n_re, n_rp, n_mode, chunks, width = sizes
    re_local, modes, pairs = coupling.shape[1], coupling.shape[2], coupling.shape[4]
    k_local = out.shape[1]
    base, left, shared, rows = segments(modes)
    tall = 2 * base + shared
    half = n_rp // CORES // 2
    me_re, me_rp, me_mode = lax.axis_index("re"), lax.axis_index("rp"), lax.axis_index("mode")
    chip, core = me_rp // CORES, me_rp % CORES
    side = jnp.where(chip >= half, 1, 0)
    depth = jnp.where(side == 1, chip - half, half - 1 - chip)

    fetches = []
    for p in range(0, pairs, LANES):
        span = pl.ds(p, min(LANES, pairs - p))
        fetches.append(pltpu.make_async_copy(
            coupling.at[:, :, :, 0, span], held.at[:, :, :, span], load.at[len(fetches)]
        ))
    for fetch in fetches:
        fetch.start()
    fetched = []

    def chip_at(d, s):
        return jnp.where(s == 1, half + d, half - 1 - d)

    inner = jnp.where(depth == 0, chip_at(0, 1 - side), chip_at(depth - 1, side)) * CORES + core
    outer = chip_at(jnp.minimum(depth + 1, half - 1), side) * CORES + core
    sibling = chip * CORES + 1 - core
    re_peers = [lax.rem(me_re + d, n_re) for d in range(1, n_re)]
    mode_peers = [lax.rem(me_mode + d, n_mode) for d in range(1, n_mode)]

    def remote(src, dst, send, recv, where):
        return pltpu.make_async_remote_copy(
            src_ref=src, dst_ref=dst, send_sem=send, recv_sem=recv,
            device_id=where, device_id_type=MESH,
        )

    def x_copy(d, j):
        return remote(xout.at[d, j], xin.at[d, j], xs.at[d, j], xr.at[d, j], {"re": re_peers[d]})

    def raw_copy(tt, i, j):
        to = half + i if tt == 0 else i + 1
        return remote(raw.at[i, j], raw.at[to, j], rs.at[i, j], rr.at[to, j], {"rp": inner})

    def raw_arrival(i, j):
        return remote(raw.at[i, j], raw.at[i, j], rs.at[0, j], rr.at[i, j], {"rp": inner})

    def sum_copy(i, j):
        return remote(sumout.at[i, j], sumin.at[i, j], ss.at[i, j], sr.at[i, j], {"rp": outer})

    def sum_arrival(i, j):
        return remote(sumin.at[i, j], sumin.at[i, j], ss.at[0, j], sr.at[i, j], {"rp": outer})

    def sib_copy(tt, j):
        some = pl.ds(0, half - tt)
        return remote(sibout.at[j, some], sibin.at[j, some], bs.at[j], br.at[j], {"rp": sibling})

    def y_copy(d, j):
        return remote(
            yout.at[mode_peers[d], j], yin.at[d, j], ys.at[d, j], yr.at[d, j],
            {"mode": mode_peers[d]},
        )

    barrier = pltpu.get_barrier_semaphore()

    def greet(where):
        pl.semaphore_signal(barrier, inc=1, device_id=where, device_id_type=MESH)

    for p in re_peers:
        greet({"re": p})
    for p in mode_peers:
        greet({"mode": p})
    greet({"rp": sibling})
    greet({"rp": inner})

    @pl.when(depth < half - 1)
    def _():
        greet({"rp": outer})

    def table(points, point, cells, first, count, cos_t, sin_t):
        for i in range(points):
            for s in range(count):
                turns = point(i, 0) * cells[0, first + s]
                for axis in range(1, cells.shape[0]):
                    turns = turns + point(i, axis) * cells[axis, first + s]
                cos_t[i, s] = roots[turns & (KG - 1)]
                sin_t[i, s] = roots[(turns + (KG - KG // 4)) & (KG - 1)]

    table(cos_e.shape[0], lambda i, a: kpoints[i, a], electron_cells, me_re * re_local, re_local, cos_e, sin_e)

    friends = n_re - 1 + n_mode - 1 + 2
    pl.semaphore_wait(barrier, friends + jnp.where(depth < half - 1, 1, 0))

    def electron(owner, j, dst):
        if left and 2 * left != shared:
            dst[base:base + shared, :] = jnp.zeros((shared, width), jnp.float32)
        spans = [(rows[0], rows[1])] + ([(rows[2], rows[3])] if left else [])
        for k, p0, p1, at in pieces_of(j, width, pairs):
            row = owner * k_local + k
            while len(fetched) * LANES < p1:
                fetches[len(fetched)].wait()
                fetched.append(p1)
            for (_, r0, r1, to_real), (_, _, _, to_imag) in spans:
                real = imag = None
                for r in range(re_local):
                    c, s = cos_e[row, r], sin_e[row, r]
                    a = held[0, r, r0:r1, p0:p1]
                    b = held[1, r, r0:r1, p0:p1]
                    x, y = c * a - s * b, c * b + s * a
                    real = x if real is None else real + x
                    imag = y if imag is None else imag + y
                dst[to_real:to_real + r1 - r0, at:at + p1 - p0] = real
                dst[to_imag:to_imag + r1 - r0, at:at + p1 - p0] = imag

    def phonon(dst, q, terms):
        factors = [(src, s_chip * CORES + core) for src, s_chip in terms]
        real = imag = both = None
        for src, s_at in factors:
            c, s = cos_p[q, s_at], sin_p[q, s_at]
            a, b = src[0:base, :], src[base + shared:tall, :]
            x, y = c * a - s * b, c * b + s * a
            real = x if real is None else real + x
            imag = y if imag is None else imag + y
        dst[0:base, :] = real
        dst[base + shared:tall, :] = imag
        if left:
            place = lax.broadcasted_iota(jnp.int32, (shared, width), 0)
            sign = jnp.where(place < shared // 2, -1.0, 1.0)
            for src, s_at in factors:
                c, s = cos_p[q, s_at], sin_p[q, s_at]
                t = src[base:base + shared, :]
                x = c * t + s * (sign * pltpu.roll(t, shared // 2, 0))
                both = x if both is None else both + x
            dst[base:base + shared, :] = both

    def peer_stage(j):
        for d in range(n_re - 1):
            electron(re_peers[d], j, xout.at[d, j])
            x_copy(d, j).start()

    for j in range(min(LEAD, chunks)):
        peer_stage(j)

    table(cos_p.shape[0], lambda i, a: qpoints[a, i], phonon_cells, 0, n_rp, cos_p, sin_p)

    def x_stage(j):
        electron(me_re, j, raw.at[0, j])
        for d in range(n_re - 1):
            x_copy(d, j).wait_recv()
        total = raw[0, j]
        for d in range(n_re - 1):
            total = total + xin[d, j]
        raw[0, j] = total
        for tt in range(half):
            @pl.when(depth == tt)
            def _():
                raw_copy(tt, 0, j).start()
        if j + LEAD < chunks:
            peer_stage(j + LEAD)

    def forward_stage(j):
        for tt in range(half - 1):
            @pl.when(depth == tt)
            def _():
                for i in range(1, half - tt):
                    raw_arrival(i, j).wait_recv()
                    raw_copy(tt, i, j).start()

    def turn_stage():
        square[...] = jnp.zeros_like(square)
        n_all = vectors.shape[3]
        flipped = []
        for part in range(2):
            square[0:modes, 0:n_all] = vectors[0, :, part, :]
            flipped.append(jnp.transpose(square[...]))
        for m in range(n_mode):
            turn[m] = jnp.zeros(turn.shape[1:], jnp.float32)
            for to, n0, n1, at_n in rows:
                for come, c0, c1, at_c in rows:
                    block = flipped[0 if to == come else 1]
                    block = block[m * modes + n0:m * modes + n1, c0:c1]
                    if to < come:
                        block = -block
                    turn[m, at_n:at_n + n1 - n0, at_c:at_c + c1 - c0] = block

    def z_stage(j):
        for tt in range(half):
            @pl.when(depth == tt)
            def _():
                own = (raw.at[0, j], chip)
                outside = [(raw.at[i, j], chip_at(tt + i, side)) for i in range(1, half - tt)]
                across = []
                if tt == 0:
                    for i in range(half):
                        raw_arrival(half + i, j).wait_recv()
                    across = [(raw.at[half + i, j], chip_at(i, 1 - side)) for i in range(half)]
                for dst, c in ((sibout, 1 - core), (mine, core)):
                    for i in range(half - tt):
                        q = chip_at(tt + i, side) * CORES + c
                        phonon(dst.at[j, i], q, [own] + across + (outside if i == 0 else []))
                    if dst is sibout:
                        sib_copy(tt, j).start()

    def sum_stage(j):
        for tt in range(half):
            @pl.when(depth == tt)
            def _():
                sib_copy(tt, j).wait_recv()
                if tt > 0:
                    for i in range(half - tt):
                        sum_arrival(i, j).wait_recv()
                for i in list(range(1, half - tt)) + [0]:
                    total = mine[j, i] + sibin[j, i]
                    if tt > 0:
                        total = total + sumin[i, j]
                    if i == 0:
                        packed[j] = total
                    else:
                        sumout[i - 1, j] = total
                        sum_copy(i - 1, j).start()

    def mode_stage(j):
        w_high, w_low = split(turn[...].reshape(n_mode * tall, tall))
        x_high, x_low = split(packed[j])

        def product(w, x):
            return jnp.dot(w, x, preferred_element_type=jnp.float32)

        turned = product(w_high, x_low) + product(w_low, x_high) + product(w_high, x_high)
        yout[:, j] = turned.reshape(n_mode, tall, width)
        for d in range(n_mode - 1):
            y_copy(d, j).start()

    def out_stage(j):
        for d in range(n_mode - 1):
            y_copy(d, j).wait_recv()
        total = yout[me_mode, j]
        for d in range(n_mode - 1):
            total = total + yin[d, j]
        for k, p0, p1, at in pieces_of(j, width, pairs):
            for part, n0, n1, at_n in rows:
                out[n0:n1, k, part, p0:p1] = total[at_n:at_n + n1 - n0, at:at + p1 - p0]

    xs_done = forwarded = 0
    turn_ready = False
    for j in range(chunks + 3):
        until = chunks
        while xs_done < until:
            x_stage(xs_done)
            xs_done += 1
            while forwarded < xs_done - 1:
                forward_stage(forwarded)
                forwarded += 1
        if xs_done == chunks and forwarded < chunks:
            forward_stage(forwarded)
            forwarded += 1
        if not turn_ready:
            turn_stage()
            turn_ready = True
        if j < chunks:
            z_stage(j)
        if 1 <= j <= chunks:
            sum_stage(j - 1)
            mode_stage(j - 1)
        if 3 <= j:
            out_stage(j - 3)

    for j in range(chunks):
        for d in range(n_re - 1):
            x_copy(d, j).wait_send()
        for d in range(n_mode - 1):
            y_copy(d, j).wait_send()
        for tt in range(half):
            @pl.when(depth == tt)
            def _():
                sib_copy(tt, j).wait_send()
                for i in range(half - tt):
                    raw_copy(tt, i, j).wait_send()
                for i in range(half - 1 - tt):
                    sum_copy(i, j).wait_send()


def shards(
    coupling, electron_cells, phonon_cells, kpoint_index, qpoint_index, eigenvectors, frequencies
):
    n_re, n_rp, n_mode = lax.axis_size("re"), lax.axis_size("rp"), lax.axis_size("mode")
    modes, pairs = coupling.shape[3], coupling.shape[4]
    k_all, q_all = kpoint_index.shape[0], qpoint_index.shape[0]
    k_local = k_all // n_re
    columns = k_local * pairs
    chunks = CHUNKS if columns % (CHUNKS * LANES) == 0 else 1
    width = columns // chunks
    base, _, shared, _ = segments(modes)
    tall = 2 * base + shared
    half = n_rp // CORES // 2
    side = -(-eigenvectors.shape[3] // LANES) * LANES
    roots = jnp.asarray(np.cos(np.arange(KG) * (2.0 * np.pi / KG)).astype(np.float32))

    block = (tall, width)
    smem = pl.BlockSpec(memory_space=pltpu.SMEM)
    vmem = pl.BlockSpec(memory_space=pltpu.VMEM)
    peers, others = max(n_re - 1, 1), max(n_mode - 1, 1)
    dma = pltpu.SemaphoreType.DMA
    rest = max(half - 1, 1)
    f32 = jnp.float32
    rotated = pl.pallas_call(
        functools.partial(kernel, (n_re, n_rp, n_mode, chunks, width)),
        out_shape=jax.ShapeDtypeStruct((modes, k_local, 2, pairs), f32),
        in_specs=[pl.BlockSpec(memory_space=pl.ANY)] + [smem] * 5 + [vmem],
        out_specs=vmem,
        scratch_shapes=[
            pltpu.VMEM((2, coupling.shape[1], modes, pairs), f32),
            pltpu.SMEM((k_all, coupling.shape[1]), f32),
            pltpu.SMEM((k_all, coupling.shape[1]), f32),
            pltpu.SMEM((q_all, n_rp), f32),
            pltpu.SMEM((q_all, n_rp), f32),
            pltpu.VMEM((side, side), f32),
            pltpu.VMEM((n_mode, tall, tall), f32),
            pltpu.VMEM((peers, chunks) + block, f32),
            pltpu.VMEM((peers, chunks) + block, f32),
            pltpu.VMEM((2 * half, chunks) + block, f32),
            pltpu.VMEM((rest, chunks) + block, f32),
            pltpu.VMEM((half, chunks) + block, f32),
            pltpu.VMEM((chunks, half) + block, f32),
            pltpu.VMEM((chunks, half) + block, f32),
            pltpu.VMEM((chunks, half) + block, f32),
            pltpu.VMEM((chunks,) + block, f32),
            pltpu.VMEM((n_mode, chunks) + block, f32),
            pltpu.VMEM((others, chunks) + block, f32),
            dma((-(-pairs // LANES),)), dma((peers, chunks)), dma((peers, chunks)),
            dma((half, chunks)), dma((2 * half, chunks)),
            dma((rest, chunks)), dma((half, chunks)),
            dma((chunks,)), dma((chunks,)),
            dma((others, chunks)), dma((others, chunks)),
        ],
        compiler_params=pltpu.CompilerParams(
            collective_id=0, has_side_effects=True, vmem_limit_bytes=56 * 1024 * 1024
        ),
    )(
        coupling.transpose(0, 1, 3, 2, 4), electron_cells.T, phonon_cells.T, kpoint_index,
        qpoint_index.T, roots, eigenvectors.transpose(0, 2, 1, 3),
    )
    factor = lax.rsqrt(2.0 * frequencies).T[:, :, None, None, None]
    return rotated[:, None] * factor


def solution(mesh):
    placed = (
        P(None, "re", "rp", "mode", None),
        P(),
        P(),
        P(),
        P(),
        P("rp", None, "mode", None),
        P("rp", "mode"),
    )
    return jax.shard_map(
        shards,
        mesh=mesh,
        in_specs=placed,
        out_specs=P("mode", "rp", "re", None, None),
        check_vma=False,
    )
```
